512 devices in a mesh: req: 4 (over z_hi), vocab: 128 (over x, z_lo, y, core).
Axes of the slice: x: 4, y: 8, z: 8 (z_hi: 4, z_lo: 2; z = z_hi * 2 + z_lo), core: 2. Of those that a mesh axis runs over, the one named last changes fastest.
Arguments:
- hidden_states: bfloat16 [1536, 8192], P('req', 'vocab'), may hold values from -260 to 260
- head_weight: bfloat16 [8192, 64128], P('req', 'vocab'), may hold values from -0.044194174 to 0.044194174
- draft_logits: bfloat16 [1536, 64128], P(('req', 'vocab')), may hold values from -350 to 350
- draft_ids: int32 [1536], P('req'), may hold values from 0 to 64127
Outputs:
- target_logprob: float32 [1536, 64128], P('req', 'vocab')
- residual: float32 [1536, 64128], P('req', 'vocab')
- accept: float32 [1536], P('req')
The draws below stay inside these ranges and needn't reach their ends.
All inputs are finite; a program needn't handle non-finite values.
Results may differ from the reference program's by a relative error of at most 0.0004.
Values may be sent and summed in bfloat16 or wider, within the bound.
No kernel may reach another device: no remote copies, remote signals or barrier semaphores. Data moves between devices by JAX's collectives and lax.ppermute only.
A program may use at most 64 MiB of HBM per device.

```python
import math
import jax
import jax.numpy as jnp

D = 8192
VOCAB = 64128
ROWS = 1536


def scaled_rows(key, shape, lowest, highest):
    first, second = jax.random.split(key)
    scales = jnp.exp(jax.random.uniform(first, (shape[0], 1), jnp.float32, math.log(lowest), math.log(highest)))
    base = jnp.clip(jax.random.normal(second, shape, jnp.float32), -6.0, 6.0)
    return base * scales


def shared_hidden(key, lowest, highest):
    rows_key, close_key, pick_key = jax.random.split(jax.random.fold_in(key, 31), 3)
    values = scaled_rows(rows_key, (ROWS, D), lowest, highest)
    selected = jax.random.permutation(pick_key, ROWS)[:ROWS // 4]
    close = scaled_rows(close_key, (ROWS // 4, D), 2.0, 6.0)
    values = values.at[selected].set(close)
    return (values.astype(jnp.bfloat16), selected)


def shared_weight(key):
    weight_key = jax.random.fold_in(key, 47)
    values = jnp.clip(jax.random.normal(weight_key, (D, VOCAB), jnp.float32), -4.0, 4.0) * D ** (-0.5)
    return values.astype(jnp.bfloat16)


def draw_hidden_states(key, part):
    values, selected = shared_hidden(key, 3.0, 8.0)
    return values


def draw_head_weight(key, part):
    return shared_weight(key)


def draw_draft_logits(key, part):
    weight = shared_weight(key)
    hidden, selected = shared_hidden(key, 3.0, 8.0)
    key = jax.random.fold_in(key, 2)
    base_key, noise_key = jax.random.split(key)
    values = scaled_rows(base_key, (ROWS, VOCAB), 2.0, 6.0)
    noise = 0.3 * jnp.clip(jax.random.normal(noise_key, (ROWS // 4, VOCAB), jnp.float32), -6.0, 6.0)
    near = jnp.dot(hidden[selected], weight, preferred_element_type=jnp.float32) + noise
    values = values.at[selected].set(near)
    return values.astype(jnp.bfloat16)


def set_ends(result, key, smallest, high):
    longest = result.shape.index(max(result.shape))
    spots = []
    for shift in (0, 1):
        where = [jax.random.randint(jax.random.fold_in(key, axis), (), 0, length) for axis, length in enumerate(result.shape)]
        where[longest] = (where[longest] + shift) % result.shape[longest]
        spots.append(tuple(where))
    return result.at[spots[0]].set(smallest).at[spots[1]].set(high)


def setup_inputs(seed: int = 0) -> dict:
    arg_keys = jax.random.split(jax.random.key(seed), 5)
    return {
        "hidden_states": draw_hidden_states(jax.random.fold_in(arg_keys[4], 71), 0),
        "head_weight": draw_head_weight(jax.random.fold_in(arg_keys[4], 71), 0),
        "draft_logits": draw_draft_logits(jax.random.fold_in(arg_keys[4], 71), 0),
        "draft_ids": set_ends(jax.random.randint(arg_keys[3], (ROWS,), 0, VOCAB), jax.random.fold_in(arg_keys[3], 1), 0, VOCAB - 1).astype(jnp.int32),
    }


def log_normalize(values):
    peak = jnp.max(values, axis=1, keepdims=True)
    total = jnp.sum(jnp.exp(values - peak), axis=1, keepdims=True)
    return values - peak - jnp.log(total)


def reference(hidden_states, head_weight, draft_logits, draft_ids):
    logits = jnp.dot(hidden_states, head_weight, preferred_element_type=jnp.float32)
    target_logprob = log_normalize(logits)
    draft_logprob = log_normalize(draft_logits.astype(jnp.float32))
    raw = jnp.maximum(jnp.exp(target_logprob) - jnp.exp(draft_logprob), 0.0)
    residual = raw / jnp.sum(raw, axis=1, keepdims=True)
    picked = draft_ids.astype(jnp.int32)[:, None]
    target_at = jnp.take_along_axis(target_logprob, picked, axis=1)[:, 0]
    draft_at = jnp.take_along_axis(draft_logprob, picked, axis=1)[:, 0]
    accept = jnp.exp(jnp.minimum(target_at - draft_at, 0.0))
    return target_logprob, residual, accept
```

```python
import jax
import jax.numpy as jnp
from jax import lax
from jax.sharding import Mesh, PartitionSpec as P

VOCAB_AXES = ("x", "zl", "y", "core")
SIZES = {"req": 4, "x": 4, "zl": 2, "y": 8, "core": 2}
GROUPS = 4
LANES = 128


def three_parts(value):
    high = lax.reduce_precision(value, 8, 7)
    middle = lax.reduce_precision(value - high, 8, 7)
    low = value - high - middle
    return jnp.stack([high, middle, low], axis=-1).astype(jnp.bfloat16)


def to_all(value):
    copies = jnp.broadcast_to(value[None], (LANES,) + value.shape)
    return lax.all_to_all(copies, VOCAB_AXES, split_axis=0, concat_axis=0, tiled=True)


def shift(value, by):
    return lax.ppermute(value, "req", [(i, (i + by) % GROUPS) for i in range(GROUPS)])


def body(hidden_states, head_weight, draft_logits, draft_ids):
    hidden = hidden_states.T
    weight = head_weight.T
    columns = weight.shape[0]
    half = 256

    swap = [(q * 4 + x, x * 4 + (q - x) % 4) for q in range(4) for x in range(4)]
    moved = lax.ppermute(hidden, ("req", "x"), swap)
    slabs = lax.all_gather(moved, "x", axis=0)

    rows = draft_logits.astype(jnp.float32)
    peak = jnp.max(rows, axis=1)
    log_total = jnp.log(jnp.sum(jnp.exp(rows - peak[:, None]), axis=1)) + peak
    count = draft_logits.shape[0]
    pieces = jnp.broadcast_to(three_parts(log_total)[:, None, :], (count, LANES, 3))
    payload = jnp.concatenate([draft_logits.reshape(count, LANES, columns), pieces], axis=2)
    received = lax.all_to_all(payload, VOCAB_AXES, split_axis=1, concat_axis=0, tiled=True)
    received = received.reshape(count * LANES, columns + 3)
    drafts = received[:, :columns].T.astype(jnp.float32)
    draft_log = jnp.sum(received[:, columns:].astype(jnp.float32), axis=1)

    def partial(k):
        slab = lax.all_gather(slabs[k], ("zl", "y", "core"), axis=0, tiled=True)
        return jnp.dot(weight, slab, preferred_element_type=jnp.float32)

    far = partial(2)
    first = shift(far[:half], 1)
    second = shift(far[half:], -1)
    up = partial(1)
    down = partial(3)
    up = jnp.concatenate([up[:half] + first, up[half:]], axis=0)
    down = jnp.concatenate([down[:half], down[half:] + second], axis=0)
    from_below = shift(up, 1)
    from_above = shift(down, -1)
    logits = partial(0) + from_below + from_above

    local_peak = jnp.max(logits, axis=0)
    local_log = jnp.log(jnp.sum(jnp.exp(logits - local_peak[None]), axis=0)) + local_peak
    logs = to_all(local_log)
    top = jnp.max(logs, axis=0)
    target_log = jnp.log(jnp.sum(jnp.exp(logs - top[None]), axis=0)) + top

    target_logprob = logits - target_log[None]
    draft_logprob = drafts - draft_log[None]
    raw = jnp.maximum(jnp.exp(target_logprob) - jnp.exp(draft_logprob), 0.0)
    positions = lax.axis_index(VOCAB_AXES) * columns + lax.broadcasted_iota(jnp.int32, (columns, 1), 0)
    chosen = draft_ids[None, :] == positions
    ratio = jnp.sum(jnp.where(chosen, target_logprob - draft_logprob, 0.0), axis=0)
    mass, ratio = jnp.sum(to_all(jnp.stack([jnp.sum(raw, axis=0), ratio])), axis=0)
    residual = raw / mass[None]
    accept = jnp.exp(jnp.minimum(ratio, 0.0))
    return (target_logprob.T, residual.T, accept)


def solution(mesh):
    fine = Mesh(mesh.devices.reshape(tuple(SIZES.values())), tuple(SIZES))
    return jax.shard_map(
        body,
        mesh=fine,
        in_specs=(P("req", VOCAB_AXES), P("req", VOCAB_AXES), P(("req",) + VOCAB_AXES, None), P("req")),
        out_specs=(P("req", VOCAB_AXES), P("req", VOCAB_AXES), P("req")),
        check_vma=False,
    )
```

```python
import jax
import jax.numpy as jnp
from jax import lax
from jax.sharding import Mesh, PartitionSpec as P

VOCAB_AXES = ("x", "zl", "y", "core")
SIZES = {"req": 4, "x": 4, "zl": 2, "y": 8, "core": 2}
GROUPS = 4
LANES = 128
DEPTH_FLIP, ROWS_FLIP = 1, 3


def three_parts(value):
    high = lax.reduce_precision(value, 8, 7)
    middle = lax.reduce_precision(value - high, 8, 7)
    low = value - high - middle
    return jnp.stack([high, middle, low], axis=-1).astype(jnp.bfloat16)


def to_all(value):
    copies = jnp.broadcast_to(value[None], (LANES,) + value.shape)
    return lax.all_to_all(copies, VOCAB_AXES, split_axis=0, concat_axis=0, tiled=True)


def pairs_over_req(flip):
    return [(i, i ^ flip) for i in range(GROUPS)]


def block_moves():
    moves, crossed = [], []
    for q in range(GROUPS):
        for x in range(GROUPS):
            (r,) = {q, q ^ ROWS_FLIP} & {x, x ^ DEPTH_FLIP}
            slot = 2 * (q != r) + (x != r)
            for zl in range(2):
                source = (q * GROUPS + x) * 2 + zl
                moves.append((source, (r * GROUPS + slot) * 2 + zl))
                crossed.append((source, (r * GROUPS + slot) * 2 + 1 - zl))
    return moves, crossed


def body(hidden_states, head_weight, draft_logits, draft_ids):
    hidden = hidden_states.T
    weight = head_weight.T
    columns, depth = weight.shape
    half = 256

    moves, crossed = block_moves()
    same = lax.ppermute(hidden, ("req", "x", "zl"), moves)
    other = lax.ppermute(hidden, ("req", "x", "zl"), crossed)
    weight, same, other = lax.optimization_barrier((weight, same, other))
    second = [lax.ppermute(part, "req", pairs_over_req(DEPTH_FLIP)) for part in (weight[:half], weight[half:])]
    first_half = lax.axis_index("zl") == 0
    unit = jnp.stack([jnp.where(first_half, same, other), jnp.where(first_half, other, same)])
    blocks = lax.all_to_all(
        jnp.broadcast_to(unit[None], (GROUPS,) + unit.shape), "x", split_axis=0, concat_axis=0, tiled=True
    )
    gathered = lax.all_gather(blocks, ("y", "core"), axis=0)
    gathered = gathered.transpose(1, 2, 0, 3, 4).reshape(GROUPS, depth, hidden.shape[1])

    rows = draft_logits.astype(jnp.float32)
    peak = jnp.max(rows, axis=1)
    log_total = jnp.log(jnp.sum(jnp.exp(rows - peak[:, None]), axis=1)) + peak
    count = draft_logits.shape[0]
    pieces = jnp.broadcast_to(three_parts(log_total)[:, None, :], (count, LANES, 3))
    payload = jnp.concatenate([draft_logits.reshape(count, LANES, columns), pieces], axis=2)
    received = lax.all_to_all(payload, VOCAB_AXES, split_axis=1, concat_axis=0, tiled=True)
    received = received.reshape(count * LANES, columns + 3)
    drafts = received[:, :columns].T.astype(jnp.float32)
    draft_log = jnp.sum(received[:, columns:].astype(jnp.float32), axis=1)

    def dot(left, right):
        return jnp.dot(left, right, preferred_element_type=jnp.float32)

    pieces = []
    for own, received_part in zip((weight[:half], weight[half:]), second):
        away = dot(own, gathered[2]) + dot(received_part, gathered[3])
        here = dot(own, gathered[0]) + dot(received_part, gathered[1])
        pieces.append(here + lax.ppermute(away, "req", pairs_over_req(ROWS_FLIP)))
    logits = jnp.concatenate(pieces, axis=0)

    local_peak = jnp.max(logits, axis=0)
    local_log = jnp.log(jnp.sum(jnp.exp(logits - local_peak[None]), axis=0)) + local_peak
    logs = to_all(local_log)
    top = jnp.max(logs, axis=0)
    target_log = jnp.log(jnp.sum(jnp.exp(logs - top[None]), axis=0)) + top

    target_logprob = logits - target_log[None]
    draft_logprob = drafts - draft_log[None]
    raw = jnp.maximum(jnp.exp(target_logprob) - jnp.exp(draft_logprob), 0.0)
    positions = lax.axis_index(VOCAB_AXES) * columns + lax.broadcasted_iota(jnp.int32, (columns, 1), 0)
    chosen = draft_ids[None, :] == positions
    ratio = jnp.sum(jnp.where(chosen, target_logprob - draft_logprob, 0.0), axis=0)
    mass, ratio = jnp.sum(to_all(jnp.stack([jnp.sum(raw, axis=0), ratio])), axis=0)
    residual = raw / mass[None]
    accept = jnp.exp(jnp.minimum(ratio, 0.0))
    return (target_logprob.T, residual.T, accept)


def solution(mesh):
    fine = Mesh(mesh.devices.reshape(tuple(SIZES.values())), tuple(SIZES))
    return jax.shard_map(
        body,
        mesh=fine,
        in_specs=(P("req", VOCAB_AXES), P("req", VOCAB_AXES), P(("req",) + VOCAB_AXES, None), P("req")),
        out_specs=(P("req", VOCAB_AXES), P("req", VOCAB_AXES), P("req")),
        check_vma=False,
    )
```

```python
import functools

import jax
import jax.numpy as jnp
from jax import lax
from jax.experimental import pallas as pl
from jax.experimental.pallas import tpu as pltpu
from jax.sharding import Mesh, PartitionSpec as P

SIZES = {"req": 4, "x": 4, "zl": 2, "y": 8, "core": 2}
VOCAB_AXES = ("x", "zl", "y", "core")
LEVELS = ((("x", "zl"), 8), (("y", "core"), 16))
GROUPS = 4
LANES = 128
DEPTH_FLIP, ROWS_FLIP = 1, 3
CUTS = (48, 352)
STEPS = 4


def three_parts(value):
    high = lax.reduce_precision(value, 8, 7)
    middle = lax.reduce_precision(value - high, 8, 7)
    low = value - high - middle
    return jnp.stack([high, middle, low], axis=-1).astype(jnp.bfloat16)


def to_all(value, axes, count):
    copies = jnp.broadcast_to(value[None], (count,) + value.shape)
    return lax.all_to_all(copies, axes, split_axis=0, concat_axis=0, tiled=True)


def over_vocab(value, combine):
    for axes, count in LEVELS:
        value = combine(to_all(value, axes, count))
    return value


def over_req(value, flip):
    return lax.ppermute(value, "req", [(i, i ^ flip) for i in range(GROUPS)])


def block_moves():
    moves = []
    for q in range(GROUPS):
        for x in range(GROUPS):
            (r,) = {q, q ^ ROWS_FLIP} & {x, x ^ DEPTH_FLIP}
            moves.append((q * GROUPS + x, r * GROUPS + 2 * (q != r) + (x != r)))
    return moves


def log_sum(logs):
    top = jnp.max(logs, axis=0)
    return top + jnp.log(jnp.sum(jnp.exp(logs - top[None]), axis=0))


def product_kernel(halves, parts, started, *refs):
    weights, refs = refs[: 2 * halves * parts], refs[2 * halves * parts :]
    slots, refs = refs[: 2 * halves], refs[2 * halves :]
    targets = refs[-2:]

    @pl.when(pl.program_id(0) == 0)
    def _():
        for i, target in enumerate(targets):
            target[...] = refs[i][...] if started else jnp.zeros_like(target)

    left = jnp.concatenate(
        [
            jnp.concatenate([weights[first + i][...] for i in range(parts)], axis=0)
            for first in range(0, len(weights), parts)
        ],
        axis=1,
    )
    for j, target in ((1, targets[1]), (0, targets[0])):
        right = jnp.concatenate(
            [slots[2 * h + j][i, 0, zl] for h in range(halves) for zl in range(2) for i in range(slots[0].shape[0])],
            axis=0,
        )
        target[...] += jnp.dot(left, right, preferred_element_type=jnp.float32)


def product(halves, blocks, start=()):
    pieces = halves[0][0]
    count, depth = sum(piece.shape[0] for piece in pieces), pieces[0].shape[1]
    rows = blocks.shape[-1]
    width = depth // (2 * STEPS)
    whole = pl.BlockSpec((count, rows), lambda i: (0, 0))
    operands, specs = [], []
    for pieces, _, _ in halves:
        for first in (0, STEPS):
            for piece in pieces:
                operands.append(piece)
                specs.append(pl.BlockSpec((piece.shape[0], width), lambda i, first=first: (0, first + i)))
    block = (blocks.shape[0] // STEPS, 1) + blocks.shape[2:]
    for _, *slots in halves:
        for slot in slots:
            operands.append(blocks)
            specs.append(pl.BlockSpec(block, lambda i, slot=slot: (i, slot, 0, 0, 0)))
    result = jax.ShapeDtypeStruct((count, rows), jnp.float32)
    return pl.pallas_call(
        functools.partial(product_kernel, len(halves), len(pieces), bool(start)),
        grid=(STEPS,),
        in_specs=specs + [whole] * len(start),
        out_specs=[whole] * 2,
        out_shape=[result, result],
        cost_estimate=pl.CostEstimate(
            flops=4 * len(halves) * count * depth * rows,
            bytes_accessed=len(halves) * (blocks.size + 2 * count * depth),
            transcendentals=0,
        ),
        compiler_params=pltpu.CompilerParams(vmem_limit_bytes=48 * 1024 * 1024),
    )(*operands, *start)


def body(hidden_states, head_weight, draft_logits, draft_ids):
    hidden = hidden_states.T
    weight = head_weight.T
    columns = weight.shape[0]

    own = [weight[: CUTS[0]], weight[CUTS[0] : CUTS[1]], weight[CUTS[1] :]]
    moved = lax.ppermute(hidden, ("req", "x"), block_moves())
    other = [over_req(own[0], DEPTH_FLIP)]
    moved, own[1], other[0] = lax.optimization_barrier((moved, own[1], other[0]))
    other.append(over_req(own[1], DEPTH_FLIP))
    own[2], other[1] = lax.optimization_barrier((own[2], other[1]))
    other.append(over_req(own[2], DEPTH_FLIP))
    blocks = lax.all_to_all(
        jnp.broadcast_to(moved[None], (2 * GROUPS,) + moved.shape), ("x", "zl"), split_axis=0, concat_axis=0, tiled=True
    )
    blocks = blocks.reshape((GROUPS, 2) + hidden.shape)
    gathered = lax.all_gather(blocks, ("y", "core"), axis=0)

    rows = draft_logits.astype(jnp.float32)
    peak = jnp.max(rows, axis=1)
    log_total = jnp.log(jnp.sum(jnp.exp(rows - peak[:, None]), axis=1)) + peak
    count = draft_logits.shape[0]
    tail = jnp.broadcast_to(three_parts(log_total)[:, None, :], (count, LANES, 3))
    payload = jnp.concatenate([draft_logits.reshape(count, LANES, columns), tail], axis=2)

    received = lax.all_to_all(payload, VOCAB_AXES, split_axis=1, concat_axis=0, tiled=True)
    here, away = product([(own[:2], 0, 2), (other[:2], 1, 3)], gathered)
    away, received = lax.optimization_barrier((away, received))
    pieces = [here + over_req(away, ROWS_FLIP)]
    received = received.reshape(count * LANES, columns + 3)
    drafts = received[:, :columns].T.astype(jnp.float32)
    draft_log = jnp.sum(received[:, columns:].astype(jnp.float32), axis=1)
    start = product([(own[2:], 0, 2)], gathered)
    here, away = product([(other[2:], 1, 3)], gathered, start)
    pieces.append(here + over_req(away, ROWS_FLIP))
    logits = jnp.concatenate(pieces, axis=0)

    target_log = over_vocab(log_sum(logits), log_sum)

    target_logprob = logits - target_log[None]
    draft_logprob = drafts - draft_log[None]
    raw = jnp.maximum(jnp.exp(target_logprob) - jnp.exp(draft_logprob), 0.0)
    positions = lax.axis_index(VOCAB_AXES) * columns + lax.broadcasted_iota(jnp.int32, (columns, 1), 0)
    chosen = draft_ids[None, :] == positions
    ratio = jnp.sum(jnp.where(chosen, target_logprob - draft_logprob, 0.0), axis=0)
    sums = jnp.stack([jnp.sum(raw, axis=0), ratio])
    mass, ratio = over_vocab(sums, lambda parts: jnp.sum(parts, axis=0))
    residual = raw / mass[None]
    accept = jnp.exp(jnp.minimum(ratio, 0.0))
    return (target_logprob.T, residual.T, accept)


def solution(mesh):
    fine = Mesh(mesh.devices.reshape(tuple(SIZES.values())), tuple(SIZES))
    return jax.shard_map(
        body,
        mesh=fine,
        in_specs=(P("req", VOCAB_AXES), P("req", VOCAB_AXES), P(("req",) + VOCAB_AXES, None), P("req")),
        out_specs=(P("req", VOCAB_AXES), P("req", VOCAB_AXES), P("req")),
        check_vma=False,
    )
```

```python
import functools

import jax
import jax.numpy as jnp
from jax import lax
from jax.experimental import pallas as pl
from jax.experimental.pallas import tpu as pltpu
from jax.sharding import Mesh, PartitionSpec as P

SIZES = {"req": 4, "x": 4, "zl": 2, "y": 8, "core": 2}
VOCAB_AXES = ("x", "zl", "y", "core")
LEVELS = ((("x", "zl", "core"), 16), (("y",), 8))
GROUPS = 4
LANES = 128
DEPTH_FLIP, ROWS_FLIP = 1, 3
CUTS = (48, 352)
STEPS = 4


def three_parts(value):
    high = lax.reduce_precision(value, 8, 7)
    middle = lax.reduce_precision(value - high, 8, 7)
    low = value - high - middle
    return jnp.stack([high, middle, low], axis=-1).astype(jnp.bfloat16)


def to_all(value, axes, count):
    copies = jnp.broadcast_to(value[None], (count,) + value.shape)
    return lax.all_to_all(copies, axes, split_axis=0, concat_axis=0, tiled=True)


def over_vocab(value, combine):
    for axes, count in LEVELS:
        value = combine(to_all(value, axes, count))
    return value


def over_req(value, flip):
    return lax.ppermute(value, "req", [(i, i ^ flip) for i in range(GROUPS)])


def block_moves():
    moves = []
    for q in range(GROUPS):
        for x in range(GROUPS):
            (r,) = {q, q ^ ROWS_FLIP} & {x, x ^ DEPTH_FLIP}
            moves.append((q * GROUPS + x, r * GROUPS + 2 * (q != r) + (x != r)))
    return moves


def log_sum(logs):
    top = jnp.max(logs, axis=0)
    return top + jnp.log(jnp.sum(jnp.exp(logs - top[None]), axis=0))


def product_kernel(halves, parts, started, *refs):
    weights, refs = refs[: 2 * halves * parts], refs[2 * halves * parts :]
    slots, refs = refs[: 2 * halves], refs[2 * halves :]
    targets = refs[-2:]

    @pl.when(pl.program_id(0) == 0)
    def _():
        for i, target in enumerate(targets):
            target[...] = refs[i][...] if started else jnp.zeros_like(target)

    left = jnp.concatenate(
        [
            jnp.concatenate([weights[first + i][...] for i in range(parts)], axis=0)
            for first in range(0, len(weights), parts)
        ],
        axis=1,
    )
    for j, target in ((1, targets[1]), (0, targets[0])):
        right = jnp.concatenate(
            [slots[2 * h + j][i, 0, zl] for h in range(halves) for zl in range(2) for i in range(slots[0].shape[0])],
            axis=0,
        )
        target[...] += jnp.dot(left, right, preferred_element_type=jnp.float32)


def product(halves, blocks, start=()):
    pieces = halves[0][0]
    count, depth = sum(piece.shape[0] for piece in pieces), pieces[0].shape[1]
    rows = blocks.shape[-1]
    width = depth // (2 * STEPS)
    whole = pl.BlockSpec((count, rows), lambda i: (0, 0))
    operands, specs = [], []
    for pieces, _, _ in halves:
        for first in (0, STEPS):
            for piece in pieces:
                operands.append(piece)
                specs.append(pl.BlockSpec((piece.shape[0], width), lambda i, first=first: (0, first + i)))
    block = (blocks.shape[0] // STEPS, 1) + blocks.shape[2:]
    for _, *slots in halves:
        for slot in slots:
            operands.append(blocks)
            specs.append(pl.BlockSpec(block, lambda i, slot=slot: (i, slot, 0, 0, 0)))
    result = jax.ShapeDtypeStruct((count, rows), jnp.float32)
    return pl.pallas_call(
        functools.partial(product_kernel, len(halves), len(pieces), bool(start)),
        grid=(STEPS,),
        in_specs=specs + [whole] * len(start),
        out_specs=[whole] * 2,
        out_shape=[result, result],
        cost_estimate=pl.CostEstimate(
            flops=4 * len(halves) * count * depth * rows,
            bytes_accessed=len(halves) * (blocks.size + 2 * count * depth),
            transcendentals=0,
        ),
        compiler_params=pltpu.CompilerParams(vmem_limit_bytes=48 * 1024 * 1024),
    )(*operands, *start)


def body(hidden_states, head_weight, draft_logits, draft_ids):
    hidden = hidden_states.T
    weight = head_weight.T
    columns = weight.shape[0]

    own = [weight[: CUTS[0]], weight[CUTS[0] : CUTS[1]], weight[CUTS[1] :]]
    moved = lax.ppermute(hidden, ("req", "x"), block_moves())
    other = [over_req(own[0], DEPTH_FLIP)]
    moved, own[1], other[0] = lax.optimization_barrier((moved, own[1], other[0]))
    other.append(over_req(own[1], DEPTH_FLIP))
    own[2], other[1] = lax.optimization_barrier((own[2], other[1]))
    other.append(over_req(own[2], DEPTH_FLIP))
    blocks = lax.all_to_all(
        jnp.broadcast_to(moved[None], (2 * GROUPS,) + moved.shape), ("x", "zl"), split_axis=0, concat_axis=0, tiled=True
    )
    blocks = blocks.reshape((GROUPS, 2) + hidden.shape)
    gathered = lax.all_gather(blocks, ("y", "core"), axis=0)

    rows = draft_logits.astype(jnp.float32)
    peak = jnp.max(rows, axis=1)
    log_total = jnp.log(jnp.sum(jnp.exp(rows - peak[:, None]), axis=1)) + peak
    count = draft_logits.shape[0]
    tail = jnp.broadcast_to(three_parts(log_total)[:, None, :], (count, LANES, 3))
    payload = jnp.concatenate([draft_logits.reshape(count, LANES, columns), tail], axis=2)

    received = lax.all_to_all(payload, VOCAB_AXES, split_axis=1, concat_axis=0, tiled=True)
    here, away = product([(own[:2], 0, 2), (other[:2], 1, 3)], gathered)
    away, received = lax.optimization_barrier((away, received))
    pieces = [here + over_req(away, ROWS_FLIP)]
    received = received.reshape(count * LANES, columns + 3)
    drafts = received[:, :columns].T.astype(jnp.float32)
    draft_log = jnp.sum(received[:, columns:].astype(jnp.float32), axis=1)
    start = product([(own[2:], 0, 2)], gathered)
    draft_logprob = drafts - draft_log[None]
    draft_share = jnp.exp(draft_logprob)
    positions = lax.axis_index(VOCAB_AXES) * columns + lax.broadcasted_iota(jnp.int32, (columns, 1), 0)
    chosen = draft_ids[None, :] == positions
    draft_at = jnp.sum(jnp.where(chosen, draft_logprob, 0.0), axis=0)
    start, draft_share, draft_at, chosen = lax.optimization_barrier((start, draft_share, draft_at, chosen))
    here, away = product([(other[2:], 1, 3)], gathered, start)
    pieces.append(here + over_req(away, ROWS_FLIP))
    logits = jnp.concatenate(pieces, axis=0)

    local_log = log_sum(logits)
    ratio = jnp.sum(jnp.where(chosen, logits, 0.0), axis=0) - draft_at
    local_log, ratio = lax.optimization_barrier((local_log, ratio))
    target_log = over_vocab(local_log, log_sum)

    target_logprob = logits - target_log[None]
    raw = jnp.maximum(jnp.exp(target_logprob) - draft_share, 0.0)
    sums = jnp.stack([jnp.sum(raw, axis=0), ratio])
    mass, ratio = over_vocab(sums, lambda parts: jnp.sum(parts, axis=0))
    ratio = ratio - target_log
    residual = raw / mass[None]
    accept = jnp.exp(jnp.minimum(ratio, 0.0))
    return (target_logprob.T, residual.T, accept)


def solution(mesh):
    fine = Mesh(mesh.devices.reshape(tuple(SIZES.values())), tuple(SIZES))
    return jax.shard_map(
        body,
        mesh=fine,
        in_specs=(P("req", VOCAB_AXES), P("req", VOCAB_AXES), P(("req",) + VOCAB_AXES, None), P("req")),
        out_specs=(P("req", VOCAB_AXES), P("req", VOCAB_AXES), P("req")),
        check_vma=False,
    )
```

```python
import functools

import jax
import jax.numpy as jnp
from jax import lax
from jax.experimental import pallas as pl
from jax.experimental.pallas import tpu as pltpu
from jax.sharding import Mesh, PartitionSpec as P

SIZES = {"req": 4, "x": 4, "zl": 2, "y": 8, "core": 2}
VOCAB_AXES = ("x", "zl", "y", "core")
LEVELS = ((("x", "zl", "core"), 16), (("y",), 8))
GROUPS = 4
LANES = 128
DEPTH_FLIP, ROWS_FLIP = 1, 3
CUTS = (48, 352)
STEPS = 2


def three_parts(value):
    high = lax.reduce_precision(value, 8, 7)
    middle = lax.reduce_precision(value - high, 8, 7)
    low = value - high - middle
    return jnp.stack([high, middle, low], axis=-1).astype(jnp.bfloat16)


def to_all(value, axes, count):
    copies = jnp.broadcast_to(value[None], (count,) + value.shape)
    return lax.all_to_all(copies, axes, split_axis=0, concat_axis=0, tiled=True)


def over_vocab(value, combine):
    for axes, count in LEVELS:
        value = combine(to_all(value, axes, count))
    return value


def over_req(value, flip):
    return lax.ppermute(value, "req", [(i, i ^ flip) for i in range(GROUPS)])


def block_moves():
    moves = []
    for q in range(GROUPS):
        for x in range(GROUPS):
            (r,) = {q, q ^ ROWS_FLIP} & {x, x ^ DEPTH_FLIP}
            moves.append((q * GROUPS + x, r * GROUPS + 2 * (q != r) + (x != r)))
    return moves


def log_sum(logs):
    top = jnp.max(logs, axis=0)
    return top + jnp.log(jnp.sum(jnp.exp(logs - top[None]), axis=0))


def product_kernel(halves, parts, started, *refs):
    weights, refs = refs[: 2 * halves * parts], refs[2 * halves * parts :]
    slots, refs = refs[: 2 * halves], refs[2 * halves :]
    targets = refs[-2:]

    @pl.when(pl.program_id(0) == 0)
    def _():
        for i, target in enumerate(targets):
            target[...] = refs[i][...] if started else jnp.zeros_like(target)

    left = jnp.concatenate(
        [
            jnp.concatenate([weights[first + i][...] for i in range(parts)], axis=0)
            for first in range(0, len(weights), parts)
        ],
        axis=1,
    )
    for j, target in ((1, targets[1]), (0, targets[0])):
        right = jnp.concatenate(
            [slots[2 * h + j][i, 0, zl] for h in range(halves) for zl in range(2) for i in range(slots[0].shape[0])],
            axis=0,
        )
        target[...] += jnp.dot(left, right, preferred_element_type=jnp.float32)


def product(halves, blocks, start=()):
    pieces = halves[0][0]
    count, depth = sum(piece.shape[0] for piece in pieces), pieces[0].shape[1]
    rows = blocks.shape[-1]
    width = depth // (2 * STEPS)
    whole = pl.BlockSpec((count, rows), lambda i: (0, 0))
    operands, specs = [], []
    for pieces, _, _ in halves:
        for first in (0, STEPS):
            for piece in pieces:
                operands.append(piece)
                specs.append(pl.BlockSpec((piece.shape[0], width), lambda i, first=first: (0, first + i)))
    block = (blocks.shape[0] // STEPS, 1) + blocks.shape[2:]
    for _, *slots in halves:
        for slot in slots:
            operands.append(blocks)
            specs.append(pl.BlockSpec(block, lambda i, slot=slot: (i, slot, 0, 0, 0)))
    result = jax.ShapeDtypeStruct((count, rows), jnp.float32)
    return pl.pallas_call(
        functools.partial(product_kernel, len(halves), len(pieces), bool(start)),
        grid=(STEPS,),
        in_specs=specs + [whole] * len(start),
        out_specs=[whole] * 2,
        out_shape=[result, result],
        cost_estimate=pl.CostEstimate(
            flops=4 * len(halves) * count * depth * rows,
            bytes_accessed=len(halves) * (blocks.size + 2 * count * depth),
            transcendentals=0,
        ),
        compiler_params=pltpu.CompilerParams(vmem_limit_bytes=48 * 1024 * 1024),
    )(*operands, *start)


def body(hidden_states, head_weight, draft_logits, draft_ids):
    hidden = hidden_states.T
    weight = head_weight.T
    columns = weight.shape[0]

    own = [weight[: CUTS[0]], weight[CUTS[0] : CUTS[1]], weight[CUTS[1] :]]
    moved = lax.ppermute(hidden, ("req", "x"), block_moves())
    other = [over_req(own[0], DEPTH_FLIP)]
    moved, own[1], other[0] = lax.optimization_barrier((moved, own[1], other[0]))
    other.append(over_req(own[1], DEPTH_FLIP))
    own[2], other[1] = lax.optimization_barrier((own[2], other[1]))
    other.append(over_req(own[2], DEPTH_FLIP))
    blocks = lax.all_to_all(
        jnp.broadcast_to(moved[None], (2 * GROUPS,) + moved.shape), ("x", "zl"), split_axis=0, concat_axis=0, tiled=True
    )
    blocks = blocks.reshape((GROUPS, 2) + hidden.shape)
    gathered = lax.all_gather(blocks, ("y", "core"), axis=0)

    rows = draft_logits.astype(jnp.float32)
    peak = jnp.max(rows, axis=1)
    log_total = jnp.log(jnp.sum(jnp.exp(rows - peak[:, None]), axis=1)) + peak
    count = draft_logits.shape[0]
    tail = jnp.broadcast_to(three_parts(log_total)[:, None, :], (count, LANES, 3))
    payload = jnp.concatenate([draft_logits.reshape(count, LANES, columns), tail], axis=2)

    received = lax.all_to_all(payload, VOCAB_AXES, split_axis=1, concat_axis=0, tiled=True)
    here, away = product([(own[:2], 0, 2), (other[:2], 1, 3)], gathered)
    away, received = lax.optimization_barrier((away, received))
    pieces = [here + over_req(away, ROWS_FLIP)]
    start = product([(own[2:], 0, 2)], gathered)
    start, received = lax.optimization_barrier((start, received))
    received = received.reshape(count * LANES, columns + 3)
    drafts = received[:, :columns].T.astype(jnp.float32)
    draft_log = jnp.sum(received[:, columns:].astype(jnp.float32), axis=1)
    draft_logprob = drafts - draft_log[None]
    draft_share = jnp.exp(draft_logprob)
    positions = lax.axis_index(VOCAB_AXES) * columns + lax.broadcasted_iota(jnp.int32, (columns, 1), 0)
    chosen = draft_ids[None, :] == positions
    draft_at = jnp.sum(jnp.where(chosen, draft_logprob, 0.0), axis=0)
    start, draft_share, draft_at, chosen = lax.optimization_barrier((start, draft_share, draft_at, chosen))
    here, away = product([(other[2:], 1, 3)], gathered, start)
    pieces.append(here + over_req(away, ROWS_FLIP))
    logits = jnp.concatenate(pieces, axis=0)

    local_log = log_sum(logits)
    ratio = jnp.sum(jnp.where(chosen, logits, 0.0), axis=0) - draft_at
    local_log, ratio = lax.optimization_barrier((local_log, ratio))
    target_log = over_vocab(local_log, log_sum)

    target_logprob = logits - target_log[None]
    raw = jnp.maximum(jnp.exp(target_logprob) - draft_share, 0.0)
    sums = jnp.stack([jnp.sum(raw, axis=0), ratio])
    mass, ratio = over_vocab(sums, lambda parts: jnp.sum(parts, axis=0))
    ratio = ratio - target_log
    residual = raw / mass[None]
    accept = jnp.exp(jnp.minimum(ratio, 0.0))
    return (target_logprob.T, residual.T, accept)


def solution(mesh):
    fine = Mesh(mesh.devices.reshape(tuple(SIZES.values())), tuple(SIZES))
    return jax.shard_map(
        body,
        mesh=fine,
        in_specs=(P("req", VOCAB_AXES), P("req", VOCAB_AXES), P(("req",) + VOCAB_AXES, None), P("req")),
        out_specs=(P("req", VOCAB_AXES), P("req", VOCAB_AXES), P("req")),
        check_vma=False,
    )
```
